512 devices in a mesh: page: 64 (over x, z, core), tensor: 8 (over y).
Axes of the slice: x: 4, y: 8, z: 8, core: 2. Of those that a mesh axis runs over, the one named last changes fastest.
Arguments:
- queries: bfloat16 [128, 4, 8192], P('page', None, 'tensor'), may hold values from -8 to 8
- prompt_keys: bfloat16 [65536, 1024], P('page', 'tensor'), may hold values from -8 to 8
- prompt_values: bfloat16 [65536, 1024], P('page', 'tensor'), may hold values from -6 to 6
- pool_keys: bfloat16 [65536, 1024], P('page', 'tensor'), may hold values from -6 to 6
- pool_values: bfloat16 [65536, 1024], P('page', 'tensor'), may hold values from -6 to 6
- suffix_keys: bfloat16 [128, 512, 1024], P('page', None, 'tensor'), may hold values from -10 to 10
- suffix_values: bfloat16 [128, 512, 1024], P('page', None, 'tensor'), may hold values from -6 to 6
- new_keys: bfloat16 [128, 4, 1024], P('page', None, 'tensor'), may hold values from -14 to 14
- new_values: bfloat16 [128, 4, 1024], P('page', None, 'tensor'), may hold values from -6 to 6
- suffix_lengths: int32 [128], P('page'), may hold values from 1 to 512, as said below
- branch_group: int32 [128], replicated, may hold values from 0 to 15
- page_list: int32 [16, 16], replicated, may hold values from 0 to 255, as said below
- out_weight: bfloat16 [8192, 5120], P('tensor', 'page'), may hold values from -0.0625 to 0.0625
Outputs:
- projected: bfloat16 [512, 5120], P('tensor', 'page')
The draws below stay inside these ranges and needn't reach their ends.
Inputs may be any that keep to these rules, and one draw needn't show every extreme that they name: `suffix_lengths`: some branch has 512 live suffix tokens and some branch has one. `page_list`: every pool page is listed exactly once over all groups.
All inputs are finite; a program needn't handle non-finite values.
Results may differ from the reference program's by a relative error of at most 0.0058.
Values may be sent and summed in bfloat16 or wider, within the bound.
No kernel may reach another device: no remote copies, remote signals or barrier semaphores. Data moves between devices by JAX's collectives and lax.ppermute only.
A program may use at most 64 MiB of HBM per device.

```python
import math
import jax
import jax.numpy as jnp
import numpy as np
from jax import lax

D = 5120
H = 64
KVH = 8
HD = 128
STEPS = 4
PAGE = 256
GROUPS = 16
SUFFIX = 512
BRANCHES = 128
PROMPT = 65536
GPAGES = 16
POOL = 65536
N_PAGE = 64


def draw_queries(key, part):
    key = jax.random.fold_in(key, 1)
    shape = (BRANCHES, STEPS, H * HD)
    values = jnp.clip(jax.random.normal(key, shape, jnp.float32), -6.0, 6.0)
    return values.astype(jnp.bfloat16)


def draw_prompt_keys(key, part):
    key = jax.random.fold_in(key, 2)
    shape = (PROMPT, KVH * HD)
    values = jnp.clip(jax.random.normal(key, shape, jnp.float32), -6.0, 6.0)
    return values.astype(jnp.bfloat16)


def draw_suffix_lengths(key, part):
    key = jax.random.fold_in(key, 3)
    lengths = jax.random.randint(key, (BRANCHES,), 1, SUFFIX + 1)
    lengths = lengths.at[0].set(SUFFIX)
    lengths = lengths.at[BRANCHES - 1].set(1)
    return lengths.astype(jnp.int32)


def draw_page_list(key, part):
    key = jax.random.fold_in(key, 4)
    order = jax.random.permutation(key, GROUPS * GPAGES)
    return order.reshape(GROUPS, GPAGES).astype(jnp.int32)


def with_ends(values, stream_key, smallest, largest):
    longest = values.shape.index(max(values.shape))
    spots = []
    for shift in (0, 1):
        where = [jax.random.randint(jax.random.fold_in(stream_key, axis), (), 0, length) for axis, length in enumerate(values.shape)]
        where[longest] = (where[longest] + shift) % values.shape[longest]
        spots.append(tuple(where))
    return values.at[spots[0]].set(smallest).at[spots[1]].set(largest)


def shard_levels(rng, dims, cuts, low, largest):
    gain = 1.0
    for axis_at, parts in cuts:
        steps = jax.random.uniform(jax.random.fold_in(jax.random.fold_in(rng, 6), axis_at), (parts,), jnp.float32, low / len(cuts), largest / len(cuts))
        gain = gain * jnp.repeat(jnp.exp(steps), dims[axis_at] // parts).reshape((-1,) + (1,) * (len(dims) - 1 - axis_at))
    return gain


def rank_table(amount, skew):
    loads = [(1 << 20) // math.isqrt(rank ** skew) + 1 for rank in range(1, amount + 1)]
    deviation = 1 + sum(loads) // (1 << 30)
    return np.cumsum(np.array([max(1, weight // deviation) for weight in loads]))


def skewed_ids(rng, shape, number_of, lean):
    listing = rank_table(number_of, lean)
    pick = jax.random.randint(jax.random.fold_in(rng, 1), shape, 0, int(listing[number_of - 1]))
    grade = jnp.searchsorted(jnp.asarray(listing, jnp.int32), pick, side="right")
    return jax.random.permutation(jax.random.fold_in(rng, 2), number_of)[grade].astype(jnp.int32)


def noise(own_key, dims, spread, most, split=(), held_as=jnp.bfloat16):
    factor_of = shard_levels(own_key, dims, split, -0.22, 0.18) if split else 1.0
    array = jax.random.normal(own_key, dims, jnp.float32) * spread * factor_of
    return jnp.minimum(jnp.maximum(array, -most), most).astype(held_as)


def setup_inputs(seed: int = 0) -> dict:
    seeds = jax.random.split(jax.random.key(seed), 14)
    return {
        "queries": draw_queries(jax.random.fold_in(seeds[13], 71), 0),
        "prompt_keys": draw_prompt_keys(jax.random.fold_in(seeds[13], 71), 0),
        "prompt_values": noise(seeds[2], (PROMPT, KVH * HD), 1.0, 6.0, ((0, 64), (1, 8))),
        "pool_keys": noise(seeds[3], (POOL, KVH * HD), 1.0, 6.0, ((0, 64), (1, 8))),
        "pool_values": noise(seeds[4], (POOL, KVH * HD), 1.0, 6.0, ((0, 64), (1, 8))),
        "suffix_keys": noise(seeds[5], (BRANCHES, SUFFIX, KVH * HD), 2.5, 10.0, ((0, 64), (2, 8))),
        "suffix_values": noise(seeds[6], (BRANCHES, SUFFIX, KVH * HD), 1.0, 6.0, ((0, 64), (2, 8))),
        "new_keys": noise(seeds[7], (BRANCHES, STEPS, KVH * HD), 3.5, 14.0, ((0, 64), (2, 8))),
        "new_values": noise(seeds[8], (BRANCHES, STEPS, KVH * HD), 1.0, 6.0, ((0, 64), (2, 8))),
        "suffix_lengths": draw_suffix_lengths(jax.random.fold_in(seeds[13], 71), 0),
        "branch_group": with_ends(skewed_ids(seeds[10], (BRANCHES,), GROUPS, 2), jax.random.fold_in(seeds[10], 3), 0, GROUPS - 1).astype(jnp.int32),
        "page_list": draw_page_list(jax.random.fold_in(seeds[13], 71), 0),
        "out_weight": noise(seeds[12], (H * HD, D), (H * HD) ** -0.5, 0.0625, ((0, 8), (1, 64))),
    }


def partial_block(query_rows, key_rows, value_rows, allowed):
    factor = 1.0 / math.sqrt(HD)
    scores = jnp.einsum('bskgd,bnkd->bskgn', query_rows.astype(jnp.float32), key_rows.astype(jnp.float32)) * factor
    scores = jnp.where(allowed[:, :, None, None, :], scores, -jnp.inf)
    maxima = lax.optimization_barrier(jnp.max(scores, axis=-1))
    powers = jnp.exp(scores - maxima[..., None])
    totals = lax.optimization_barrier(jnp.sum(powers, axis=-1))
    rounded = lax.optimization_barrier(powers.astype(jnp.bfloat16))
    outputs = jnp.einsum('bskgn,bnkd->bskgd', rounded.astype(jnp.float32), value_rows.astype(jnp.float32))
    return (outputs, maxima, totals)

def normalize(outputs, maxima, totals):
    normed = lax.optimization_barrier((outputs / totals[..., None]).astype(jnp.bfloat16)).astype(jnp.float32)
    return (normed, maxima + jnp.log(totals))

def reference(queries, prompt_keys, prompt_values, pool_keys, pool_values, suffix_keys, suffix_values, new_keys, new_values, suffix_lengths, branch_group, page_list, out_weight):
    group_size = H // KVH
    rows_all = BRANCHES * STEPS
    branch_query = queries.reshape(BRANCHES, STEPS, KVH, group_size, HD)
    old_allowed = jnp.arange(SUFFIX)[None, None, :] < suffix_lengths[:, None, None]
    new_allowed = jnp.arange(STEPS)[None, :, None] >= jnp.arange(STEPS)[None, None, :]
    allowed = jnp.concatenate([jnp.broadcast_to(old_allowed, (BRANCHES, STEPS, SUFFIX)), jnp.broadcast_to(new_allowed, (BRANCHES, STEPS, STEPS))], axis=2)
    own_keys = jnp.concatenate([suffix_keys, new_keys], axis=1).reshape(BRANCHES, SUFFIX + STEPS, KVH, HD)
    own_values = jnp.concatenate([suffix_values, new_values], axis=1).reshape(BRANCHES, SUFFIX + STEPS, KVH, HD)
    own_out, own_max, own_total = partial_block(branch_query, own_keys, own_values, allowed)
    own_normed, own_lse = normalize(own_out, own_max, own_total)
    own_normed = own_normed.reshape(1, rows_all, KVH, group_size, HD)
    own_lse = own_lse.reshape(1, rows_all, KVH, group_size)
    page_ids = jnp.arange(GROUPS * GPAGES).astype(jnp.int32)
    matched = page_list[:, :, None] == page_ids[None, None, :]
    owner_group = lax.optimization_barrier(jnp.sum(jnp.where(matched, jnp.arange(GROUPS).astype(jnp.int32)[:, None, None], 0), axis=(0, 1))).astype(jnp.int32)
    token_group = jnp.repeat(owner_group, PAGE).reshape(N_PAGE, -1)
    row_group = jnp.repeat(branch_group, STEPS)
    query_all = queries.reshape(1, rows_all, KVH, group_size, HD)
    span = PROMPT // N_PAGE
    prompt_k = prompt_keys.reshape(N_PAGE, span, KVH, HD)
    prompt_v = prompt_values.reshape(N_PAGE, span, KVH, HD)
    pool_k = pool_keys.reshape(N_PAGE, -1, KVH, HD)
    pool_v = pool_values.reshape(N_PAGE, -1, KVH, HD)

    def fold_device(carry, piece):
        overall, denominator, summed = carry
        key_p, value_p, key_g, value_g, group_g = piece
        key_rows = jnp.concatenate([key_p, key_g], axis=0)[None]
        value_rows = jnp.concatenate([value_p, value_g], axis=0)[None]
        visible = jnp.concatenate([jnp.ones((rows_all, span), dtype=bool), row_group[:, None] == group_g[None, :]], axis=1)[None]
        outputs, maxima, totals = partial_block(query_all, key_rows, value_rows, visible)
        normed, lse = normalize(outputs, maxima, totals)
        raised = jnp.maximum(overall, lse)
        old_scale = jnp.exp(overall - raised)
        new_scale = jnp.exp(lse - raised)
        return ((raised, denominator * old_scale + new_scale, summed * old_scale[..., None] + normed * new_scale[..., None]), None)
    start = (own_lse, jnp.ones_like(own_lse), own_normed)
    (overall, denominator, summed), unused = lax.scan(fold_device, start, (prompt_k, prompt_v, pool_k, pool_v, token_group))
    attention = (summed / denominator[..., None]).astype(jnp.bfloat16).reshape(rows_all, H * HD)
    return jnp.dot(attention, out_weight, preferred_element_type=jnp.float32).astype(jnp.bfloat16)
```

```python
import functools
import math

import jax
import jax.numpy as jnp
from jax import lax
from jax.experimental import pallas as pl
from jax.experimental.pallas import tpu as pltpu
from jax.sharding import PartitionSpec as P

HD = 128
PAGE = 256
HEADS = 8
X, Z = 4, 8
CHIPS = X * Z
T = 8
ROWS = CHIPS * 8
WIDTH = HEADS * HD
PACKED = WIDTH + 128
FACTOR = 1.0 / math.sqrt(HD)
LOG2E = math.log2(math.e)
NEG = -1e30
NT = (((1,), (1,)), ((), ()))
BF16, F32 = jnp.bfloat16, jnp.float32
VMEM = pl.BlockSpec(memory_space=pltpu.VMEM)
SMEM = pl.BlockSpec(memory_space=pltpu.SMEM)


def page_id(x, z, core):
    return (x * Z + z) * 2 + core


XZ_GROUPS = [[page_id(x, z, c) for x in range(X) for z in range(Z)] for c in range(2)]
X_GROUPS = [[page_id(x, z, c) for x in range(X)] for z in range(Z) for c in range(2)]
ZT_GROUPS = [
    [page_id(x, z, c) * T + t for z in range(Z) for t in range(T)] for x in range(X) for c in range(2)
]
CORE_SWAP = [(p, p ^ 1) for p in range(2 * CHIPS)]


def split3(x):
    high = x.astype(BF16).astype(F32)
    rest = x - high
    middle = rest.astype(BF16).astype(F32)
    return high, middle, rest - middle


def attend_kernel(
    chip_ref, groups_ref, q_ref, row_group_ref, own_ref, own_lse_ref, pk_ref, pv_ref, gk_ref, gv_ref, other_ref,
    out_ref, q_rows, own_rows,
):
    source = lambda n, k: (lax.broadcasted_iota(jnp.int32, (n, k), 0) % 8) * CHIPS + (
        lax.broadcasted_iota(jnp.int32, (n, k), 0) // 8
    )
    order = (source(ROWS, ROWS) == lax.broadcasted_iota(jnp.int32, (ROWS, ROWS), 1)).astype(BF16)
    q_rows[...] = jnp.dot(order, q_ref[...], preferred_element_type=F32).astype(BF16)
    first = chip_ref[0] * 8
    place = (source(ROWS, 8) == lax.broadcasted_iota(jnp.int32, (ROWS, 8), 1) + first).astype(BF16)
    own_rows[:, :WIDTH] = jnp.dot(place, own_ref[...], preferred_element_type=F32)
    own_lse = functools.reduce(
        jnp.add,
        [jnp.dot(place, part.astype(BF16), preferred_element_type=F32) for part in split3(own_lse_ref[...])],
    )
    at = source(ROWS, 128)
    own_rows[:, WIDTH:] = jnp.where((at >= first) & (at < first + 8), own_lse, NEG)
    lane = lax.broadcasted_iota(jnp.int32, (ROWS, 128), 1)
    row_group = row_group_ref[...]
    bias = [jnp.where(row_group == groups_ref[j], 0.0, NEG) for j in range(8)]
    stats = jnp.zeros((ROWS, 128), F32)
    for h in range(HEADS):
        cols = slice(h * HD, (h + 1) * HD)
        q = q_rows[:, cols]
        keys = [pk_ref[...], other_ref[0:1024, :], gk_ref[...], other_ref[1024:2048, :]]
        values = [pv_ref[...], other_ref[2048:3072, :], gv_ref[...], other_ref[3072:4096, :]]
        scores = [lax.dot_general(q, k, NT, preferred_element_type=F32) for k in keys]
        for b in (0, 1):
            scores[2 + b] = jnp.concatenate(
                [scores[2 + b][:, j * PAGE : (j + 1) * PAGE] + bias[4 * b + j] for j in range(4)], axis=1
            )
        peak = functools.reduce(jnp.maximum, [jnp.max(s, axis=1, keepdims=True) for s in scores])
        peak = peak * (FACTOR * LOG2E)
        mass, total = 0.0, 0.0
        for s, v in zip(scores, values):
            power = jnp.exp2(s * (FACTOR * LOG2E) - peak)
            mass = mass + jnp.sum(power, axis=1, keepdims=True)
            total = total + jnp.dot(power.astype(BF16), v, preferred_element_type=F32)
        own_l = own_rows[:, WIDTH + h : WIDTH + h + 1]
        top = jnp.maximum(peak, own_l)
        scale, own_scale = jnp.exp2(peak - top), jnp.exp2(own_l - top)
        mass = mass * scale + own_scale
        total = total * scale + own_rows[:, cols] * own_scale
        out_ref[:, cols] = (total / mass).astype(BF16)
        high, middle, low = split3(top + jnp.log2(mass))
        stats = jnp.where(
            lane == h, high, jnp.where(lane == 8 + h, middle, jnp.where(lane == 16 + h, low, stats))
        )
    out_ref[:, WIDTH:] = stats.astype(BF16)


def merge_kernel(came_ref, out_ref, rows_ref):
    parts = came_ref[:, :, WIDTH:].astype(F32)
    lse = parts + pltpu.roll(parts, 120, 2) + pltpu.roll(parts, 112, 2)
    top = jnp.max(lse, axis=0, keepdims=True)
    weights = jnp.exp2(lse - top)
    weights = weights / jnp.sum(weights, axis=0, keepdims=True)
    for h in range(HEADS):
        rows = came_ref[:, :, h * HD : (h + 1) * HD].astype(F32)
        rows_ref[:, h, :] = jnp.sum(rows * weights[:, :, h : h + 1], axis=0)
    rows = rows_ref[...].astype(BF16)
    for z in range(Z):
        out_ref[z] = rows


def own_partial(queries, suffix_keys, suffix_values, new_keys, new_values, suffix_lengths):
    owned, steps, _ = queries.shape
    suffix_len = suffix_keys.shape[1]
    own_query = queries.reshape(owned, steps, HEADS, HD)
    own_keys = jnp.concatenate([suffix_keys, new_keys], axis=1)
    own_values = jnp.concatenate([suffix_values, new_values], axis=1)
    old_allowed = jnp.arange(suffix_len)[None, None, :] < suffix_lengths[:, None, None]
    new_allowed = jnp.arange(steps)[None, :, None] >= jnp.arange(steps)[None, None, :]
    allowed = jnp.concatenate(
        [
            jnp.broadcast_to(old_allowed, (owned, steps, suffix_len)),
            jnp.broadcast_to(new_allowed, (owned, steps, steps)),
        ],
        axis=2,
    )
    scores = jnp.einsum("bshd,bnd->bshn", own_query, own_keys, preferred_element_type=F32) * (FACTOR * LOG2E)
    scores = jnp.where(allowed[:, :, None, :], scores, -jnp.inf)
    maxima = jnp.max(scores, axis=-1)
    powers = jnp.exp2(scores - maxima[..., None])
    totals = jnp.sum(powers, axis=-1)
    outputs = jnp.einsum("bshn,bnd->bshd", powers.astype(BF16), own_values, preferred_element_type=F32)
    normed = (outputs / totals[..., None]).astype(BF16).reshape(owned * steps, WIDTH)
    lse = (maxima + jnp.log2(totals)).reshape(owned * steps, HEADS)
    return normed, jnp.pad(lse, ((0, 0), (0, 128 - HEADS)))


def local(
    queries,
    prompt_keys,
    prompt_values,
    pool_keys,
    pool_values,
    suffix_keys,
    suffix_values,
    new_keys,
    new_values,
    suffix_lengths,
    branch_group,
    page_list,
    out_weight,
):
    page = lax.axis_index("page")
    core, chip = page % 2, page // 2
    sent = jnp.broadcast_to(queries.reshape(1, 8, WIDTH), (CHIPS, 8, WIDTH))
    gathered = lax.all_to_all(sent, "page", 0, 0, tiled=True, axis_index_groups=XZ_GROUPS)
    gathered = gathered.reshape(ROWS, WIDTH)
    other = jnp.concatenate([prompt_keys, pool_keys, prompt_values, pool_values], axis=0)
    other = lax.ppermute(other, "page", CORE_SWAP)
    weight = lax.all_gather(out_weight, "tensor", axis=0, tiled=True)

    row_group = jnp.repeat(branch_group, 4).reshape(T, X, 2, Z)
    row_group = lax.dynamic_index_in_dim(row_group, core, 2, keepdims=False)
    row_group = row_group.transpose(1, 2, 0).reshape(ROWS, 1)
    page_ids = jnp.concatenate([page * 4 + jnp.arange(4), (page ^ 1) * 4 + jnp.arange(4)])
    matched = page_list[:, :, None] == page_ids[None, None, :]
    page_group = jnp.sum(
        jnp.where(matched, jnp.arange(page_list.shape[0])[:, None, None], 0), axis=(0, 1)
    )
    own, own_lse = own_partial(
        queries, suffix_keys, suffix_values, new_keys, new_values, suffix_lengths
    )
    packed = pl.pallas_call(
        attend_kernel,
        out_shape=jax.ShapeDtypeStruct((ROWS, PACKED), BF16),
        in_specs=[SMEM, SMEM] + [VMEM] * 9,
        out_specs=VMEM,
        scratch_shapes=[pltpu.VMEM((ROWS, WIDTH), BF16), pltpu.VMEM((ROWS, PACKED), F32)],
        compiler_params=pltpu.CompilerParams(vmem_limit_bytes=48 * 1024 * 1024),
    )(
        chip.reshape(1), page_group, gathered, row_group, own, own_lse,
        prompt_keys, prompt_values, pool_keys, pool_values, other,
    )
    came = lax.all_to_all(
        packed.reshape(CHIPS, 8, PACKED), "page", 0, 0, tiled=True, axis_index_groups=XZ_GROUPS
    )
    rows = pl.pallas_call(
        merge_kernel,
        out_shape=jax.ShapeDtypeStruct((Z, T, HEADS, HD), BF16),
        in_specs=[VMEM],
        out_specs=VMEM,
        scratch_shapes=[pltpu.VMEM((8, HEADS, HD), F32)],
    )(came)
    rows = lax.all_to_all(
        rows.reshape(Z * T, HEADS, HD), ("page", "tensor"), 0, 0, tiled=True, axis_index_groups=ZT_GROUPS
    )
    rows = jnp.broadcast_to(rows.reshape(1, Z, T * WIDTH), (X, Z, T * WIDTH))
    rows = lax.all_to_all(rows, "page", 0, 0, tiled=True, axis_index_groups=X_GROUPS)
    rows = rows.reshape(CHIPS, T * WIDTH)
    rows_other = lax.ppermute(rows, "page", CORE_SWAP)
    mine = jnp.dot(rows, weight, preferred_element_type=F32).astype(BF16).reshape(X, 1, Z, -1)
    theirs = jnp.dot(rows_other, weight, preferred_element_type=F32).astype(BF16).reshape(X, 1, Z, -1)
    both = jnp.where(
        core == 0, jnp.concatenate([mine, theirs], axis=1), jnp.concatenate([theirs, mine], axis=1)
    )
    return both.reshape(2 * CHIPS, -1)


def solution(mesh):
    placed = (
        P("page", None, "tensor"),
        P("page", "tensor"),
        P("page", "tensor"),
        P("page", "tensor"),
        P("page", "tensor"),
        P("page", None, "tensor"),
        P("page", None, "tensor"),
        P("page", None, "tensor"),
        P("page", None, "tensor"),
        P("page"),
        P(),
        P(),
        P("tensor", "page"),
    )
    return jax.shard_map(
        local, mesh=mesh, in_specs=placed, out_specs=P("tensor", "page"), check_vma=False
    )
```

```python
import functools
import math

import jax
import jax.numpy as jnp
from jax import lax
from jax.experimental import pallas as pl
from jax.experimental.pallas import tpu as pltpu
from jax.sharding import PartitionSpec as P

HD = 128
PAGE = 256
HEADS = 8
X, Z = 4, 8
CHIPS = X * Z
T = 8
ROWS = CHIPS * 8
WIDTH = HEADS * HD
PACKED = WIDTH + 128
SUFFIX = 512
SCALE = math.log2(math.e) / math.sqrt(HD)
PROMPT, KEYS = 2048, 4096
WINDOW = 64
OFFSETS = (0, 4, 2, 6, 1, 5, 7, 3)
WEIGHT_AT = ((0, 0), (0, 1), (1, 0), (2, 0), (3, 0), (3, 1), (4, 0), (4, 1))
NEG = -1e30
NT = (((1,), (1,)), ((), ()))
BF16, F32 = jnp.bfloat16, jnp.float32
VMEM = pl.BlockSpec(memory_space=pltpu.VMEM)
SMEM = pl.BlockSpec(memory_space=pltpu.SMEM)
HBM = pl.BlockSpec(memory_space=pltpu.HBM)
PARAMS = pltpu.CompilerParams(vmem_limit_bytes=60 * 1024 * 1024)
SMALL = pltpu.CompilerParams(vmem_limit_bytes=8 * 1024 * 1024)


def page_id(x, z, core):
    return (x * Z + z) * 2 + core


XZ_GROUPS = [[page_id(x, z, c) for x in range(X) for z in range(Z)] for c in range(2)]
X_GROUPS = [[page_id(x, z, c) for x in range(X)] for z in range(Z) for c in range(2)]
ZT_GROUPS = [
    [page_id(x, z, c) * T + t for z in range(Z) for t in range(T)] for x in range(X) for c in range(2)
]
CORE_SWAP = [(p, p ^ 1) for p in range(2 * CHIPS)]


def split3(x):
    high = x.astype(BF16).astype(F32)
    rest = x - high
    middle = rest.astype(BF16).astype(F32)
    return high, middle, rest - middle


def spread_kernel(q_ref, out_ref):
    rows = jnp.concatenate([q_ref[0].astype(F32), q_ref[1].astype(F32)], axis=0).astype(BF16)
    for i in range(CHIPS):
        out_ref[i] = rows


def copies_of(pairs, sems):
    return [pltpu.make_async_copy(a, b, sems.at[i]) for i, (a, b) in enumerate(pairs)]


def prep_kernel(
    chip_ref, groups_ref, lengths_ref, row_group_ref, new_keys_ref, new_values_ref, *refs,
):
    sources, results, held, made = refs[:7], refs[7:15], refs[15:25], refs[25:33]
    in_sems, out_sems = refs[33:]
    sources = sources[:4] + tuple(sources[4].at[n * 1024 : (n + 1) * 1024] for n in range(4)) + sources[5:]
    suffix_keys_ref, suffix_values_ref = held[8:]
    keys_ref, values_ref, own_keys_ref, own_values_ref, longest_ref, sort_ref, unsort_ref, marks_ref = made
    incoming = copies_of(list(zip(sources, held)), in_sems)
    quarters = [slice(n * 1024, (n + 1) * 1024) for n in range(4)]
    outgoing = copies_of(
        list(zip(made[2:], results[2:]))
        + [(made[i].at[rows], results[i].at[rows]) for rows in quarters for i in (0, 1)],
        out_sems,
    )
    for copy in incoming:
        copy.start()
    lane = lax.broadcasted_iota(jnp.int32, (PAGE, 128), 1)
    ones = jnp.ones((PAGE, HD), BF16)
    down = lax.broadcasted_iota(jnp.int32, (ROWS, ROWS), 0)
    across = lax.broadcasted_iota(jnp.int32, (ROWS, ROWS), 1)
    group_across = row_group_ref[...]
    group_down = jnp.sum(jnp.where(down == across, group_across, 0), axis=1, keepdims=True)
    before = group_down * ROWS + down < group_across * ROWS + across
    rank = jnp.sum(before.astype(jnp.int32), axis=0, keepdims=True)
    sort = (rank == down).astype(BF16)
    sort_ref[...] = sort
    order = ((down % 8) * CHIPS + down // 8 == across).astype(BF16)
    unsort_ref[...] = lax.dot_general(order, sort, NT, preferred_element_type=F32).astype(BF16)
    mark = lax.broadcasted_iota(jnp.int32, (ROWS, 128), 1)
    place = lax.broadcasted_iota(jnp.int32, (ROWS, 128), 0) - chip_ref[0] * 8
    own = (place >= 0) & (place < 8)
    marks = (mark == 16 + group_down) | (own & (mark == 32 + place)) | (jnp.logical_not(own) & (mark == 40))
    marks_ref[...] = jnp.dot(sort, marks.astype(BF16), preferred_element_type=F32)
    for copy in outgoing[3:6]:
        copy.start()
    longest = jnp.zeros((PAGE, 1), F32)
    for n, group_at in ((0, None), (2, 0), (1, None), (3, 4)):
        source = (0, 4, 2, 6)[n]
        incoming[source].wait()
        incoming[source + 1].wait()
        for j in range(4):
            rows = slice((4 * n + j) * PAGE, (4 * n + j + 1) * PAGE)
            key = held[source][j * PAGE : (j + 1) * PAGE, :]
            wide = key.astype(F32)
            longest = jnp.maximum(longest, jnp.sum(wide * wide, axis=1, keepdims=True))
            more = (lane < 8).astype(F32)
            if group_at is not None:
                hidden = (lane >= 16) & (lane < 32) & (lane != 16 + groups_ref[group_at + j])
                more = jnp.where(hidden, NEG, more)
            keys_ref[rows, :HD] = key
            keys_ref[rows, HD:] = more.astype(BF16)
            values_ref[rows, :HD] = held[source + 1][j * PAGE : (j + 1) * PAGE, :]
            values_ref[rows, HD:] = ones
        outgoing[6 + 2 * n].start()
        outgoing[7 + 2 * n].start()
    incoming[8].wait()
    incoming[9].wait()
    new_lane = lax.broadcasted_iota(jnp.int32, (16, 128), 1)
    new_token = lax.broadcasted_iota(jnp.int32, (16, 128), 0)
    blank = jnp.zeros((12, HD), F32)
    longest_own = longest
    for j in range(2):
        here = (lane >= 32 + 4 * j) & (lane < 36 + 4 * j)
        other_row = (lane >= 32) & (lane <= 40) & jnp.logical_not(here)
        for n in range(SUFFIX // PAGE):
            rows = slice(n * PAGE, (n + 1) * PAGE)
            token = lax.broadcasted_iota(jnp.int32, (PAGE, 128), 0) + n * PAGE
            hidden = other_row | (here & (token >= lengths_ref[j]))
            key = suffix_keys_ref[j, rows, :]
            wide = key.astype(F32)
            longest_own = jnp.maximum(longest_own, jnp.sum(wide * wide, axis=1, keepdims=True))
            own_keys_ref[j, rows, :HD] = key
            own_keys_ref[j, rows, HD:] = jnp.where(hidden, NEG, (lane < 8).astype(F32)).astype(BF16)
            own_values_ref[j, rows, :HD] = suffix_values_ref[j, rows, :]
            own_values_ref[j, rows, HD:] = ones
        seen = (new_lane >= 32 + 4 * j) & (new_lane < 36 + 4 * j) & (new_token <= new_lane - (32 + 4 * j))
        hidden = (new_lane >= 32) & (new_lane <= 40) & jnp.logical_not(seen)
        wide = new_keys_ref[j].astype(F32)
        longest_own = jnp.maximum(longest_own, jnp.max(jnp.sum(wide * wide, axis=1, keepdims=True)))
        own_keys_ref[j, SUFFIX:, :HD] = jnp.concatenate([wide, blank], axis=0).astype(BF16)
        own_keys_ref[j, SUFFIX:, HD:] = jnp.where(hidden, NEG, (new_lane < 8).astype(F32)).astype(BF16)
        own_values_ref[j, SUFFIX:, :HD] = jnp.concatenate([new_values_ref[j].astype(F32), blank], axis=0).astype(BF16)
        own_values_ref[j, SUFFIX:, HD:] = ones[:16]
    longest_ref[0:1, :] = jnp.broadcast_to(jnp.sqrt(jnp.max(longest)) * 1.02, (1, 128))
    longest_ref[1:2, :] = jnp.broadcast_to(jnp.sqrt(jnp.max(longest_own)) * 1.02, (1, 128))
    longest_ref[2:8, :] = jnp.zeros((6, 128), F32)
    for copy in outgoing[:3]:
        copy.start()
    for copy in outgoing:
        copy.wait()


def attend_kernel(
    at_ref, *refs,
):
    sources, out_ref, (q_rows, shift_ref, total_ref, sent_ref), held, sems = (
        refs[:9], refs[9], refs[10:14], refs[14:23], refs[23]
    )
    keys_ref, values_ref, own_keys_ref, own_values_ref, longest_ref, sort_ref, unsort_ref, marks_ref, q_ref = held
    copies = copies_of(list(zip(sources, held)), sems)
    for i in (8, 5, 7, 4, 0, 1, 2, 3, 6):
        copies[i].start()
    for i in (8, 5, 7, 4):
        copies[i].wait()
    lane = lax.broadcasted_iota(jnp.int32, (ROWS, 128), 1)
    q_all = jnp.dot(sort_ref[...], q_ref[...], preferred_element_type=F32)
    by_head = lax.broadcasted_iota(jnp.int32, (WIDTH, 128), 0) // HD == lax.broadcasted_iota(jnp.int32, (WIDTH, 128), 1)
    squares = jnp.dot((q_all * q_all).astype(BF16), by_head.astype(BF16), preferred_element_type=F32)
    marks = marks_ref[...]
    longest = jnp.where(marks[:, 40:41] > 0.5, longest_ref[0:1, :], longest_ref[1:2, :])
    shift = (jnp.sqrt(squares) * longest).astype(BF16).astype(F32)
    shift_ref[...] = shift
    for h in range(HEADS):
        q_rows[h, :, :HD] = q_all[:, h * HD : (h + 1) * HD].astype(BF16)
        q_rows[h, :, HD:] = jnp.where(lane == h, -shift, marks).astype(BF16)

    def powers(q, keys, more=0.0):
        return jnp.exp2(lax.dot_general(q, keys, NT, preferred_element_type=F32) * SCALE + more).astype(BF16)

    def taken(j, row, size, keys, values, more=0.0):
        rows = pl.ds(pl.multiple_of(row, 16), size)
        q = q_rows[:, rows, :].reshape(HEADS * size, 2 * HD)
        return rows, size, jnp.dot(powers(q, keys, more), values, preferred_element_type=F32)

    def add(rows, size, added):
        total_ref[:, rows, :] += added.reshape(HEADS, size, 2 * HD)

    def page(j):
        return pl.ds(pl.multiple_of(PROMPT + j * PAGE, PAGE), PAGE)

    for i in (0, 1, 2, 3, 6):
        copies[i].wait()
    for h in range(HEADS):
        power = powers(q_rows[h], keys_ref[:PROMPT, :])
        total_ref[h] = jnp.dot(power, values_ref[:PROMPT, :], preferred_element_type=F32)
    firsts = [jnp.minimum(lax.div(at_ref[j], 16) * 16, ROWS - WINDOW) for j in range(8)]
    parts = [taken(j, firsts[j], WINDOW, keys_ref[page(j), :], values_ref[page(j), :]) for j in range(8)]
    parts += [
        taken(j, lax.div(at_ref[16 + j], 16) * 16, 16, own_keys_ref[j], own_values_ref[j]) for j in range(2)
    ]
    for part in parts:
        add(*part)

    def rest(j, _):
        first = jnp.minimum(lax.div(at_ref[j], 16) * 16, ROWS - WINDOW) + WINDOW
        left = at_ref[8 + j] - first

        def more_rows(i, _):
            wanted = first + i * WINDOW
            row = jnp.minimum(wanted, ROWS - WINDOW)
            done = lax.broadcasted_iota(jnp.int32, (HEADS, WINDOW, 1), 1) + row < wanted
            hide = jnp.where(done, NEG, 0.0).reshape(HEADS * WINDOW, 1)
            add(*taken(j, row, WINDOW, keys_ref[page(j), :], values_ref[page(j), :], hide))
            return 0

        lax.fori_loop(0, jnp.where(left > 0, lax.div(left + WINDOW - 1, WINDOW), 0), more_rows, 0)
        return 0

    lax.fori_loop(0, 8, rest, 0)

    def masses():
        mass = jnp.ones((ROWS, 128), F32)
        for h in range(HEADS):
            mass = jnp.where(lane == h, total_ref[h, :, HD:], mass)
        return mass

    @pl.when(jnp.min(masses()) < 2.0**-90)
    def _():
        def one_head(h, _):
            def scores(keys):
                return lax.dot_general(q_rows[h], keys, NT, preferred_element_type=F32)

            def some(c):
                return pl.ds(pl.multiple_of(c * 1024, 1024), 1024)

            def peak_of(c, peak):
                return jnp.maximum(peak, jnp.max(scores(keys_ref[some(c), :]), axis=1, keepdims=True))

            peak = lax.fori_loop(0, KEYS // 1024, peak_of, jnp.full((ROWS, 1), -3e38, F32))
            for j in range(2):
                peak = jnp.maximum(peak, jnp.max(scores(own_keys_ref[j]), axis=1, keepdims=True))
            total_ref[h] = jnp.zeros((ROWS, 2 * HD), F32)

            def add_some(keys, values):
                power = jnp.exp2((scores(keys) - peak) * SCALE).astype(BF16)
                total_ref[h] += jnp.dot(power, values, preferred_element_type=F32)

            def add_chunk(c, _):
                add_some(keys_ref[some(c), :], values_ref[some(c), :])
                return 0

            lax.fori_loop(0, KEYS // 1024, add_chunk, 0)
            for j in range(2):
                add_some(own_keys_ref[j], own_values_ref[j])
            shift_ref[...] += jnp.where(lane == h, peak, 0.0)
            return 0

        lax.fori_loop(0, HEADS, one_head, 0)

    for h in range(HEADS):
        sent_ref[:, h * HD : (h + 1) * HD] = (total_ref[h, :, :HD] / total_ref[h, :, HD:]).astype(BF16)
    lse = jnp.where(lane < HEADS, shift_ref[...] * SCALE + jnp.log2(masses()), 0.0)
    high, middle, low = split3(lse)
    sent_ref[:, WIDTH:] = (high + pltpu.roll(middle, 8, 1) + pltpu.roll(low, 16, 1)).astype(BF16)
    out_ref[...] = jnp.dot(unsort_ref[...], sent_ref[...], preferred_element_type=F32).astype(BF16)


def merge_kernel(came_ref, out_ref, rows_ref):
    parts = came_ref[:, :, WIDTH:].astype(F32)
    lse = parts + pltpu.roll(parts, 120, 2) + pltpu.roll(parts, 112, 2)
    top = jnp.max(lse, axis=0, keepdims=True)
    weights = jnp.exp2(lse - top)
    weights = weights / jnp.sum(weights, axis=0, keepdims=True)
    for h in range(HEADS):
        rows = came_ref[:, :, h * HD : (h + 1) * HD].astype(F32)
        rows_ref[:, h, :] = jnp.sum(rows * weights[:, :, h : h + 1], axis=0)
    rows = rows_ref[...].astype(BF16)
    for z in range(Z):
        out_ref[z] = rows


def project(rank_ref, rows_ref, weight_refs):
    total = 0.0
    for j, offset in enumerate(OFFSETS):
        block = lax.rem(rank_ref[0] + offset, T)
        rows = rows_ref[:, pl.ds(pl.multiple_of(block * WIDTH, WIDTH), WIDTH)]
        ref, at = WEIGHT_AT[j]
        total = total + lax.dot_general(rows, weight_refs[ref][at], NT, preferred_element_type=F32)
    return total


def project_mine_kernel(rank_ref, rows_ref, w0, w1, w2, w3, w4, out_ref):
    out_ref[...] = project(rank_ref, rows_ref, (w0, w1, w2, w3, w4))


def project_all_kernel(rank_ref, core_ref, rows_ref, w0, w1, w2, w3, w4, mine_ref, out_ref):
    theirs, mine = project(rank_ref, rows_ref, (w0, w1, w2, w3, w4)), mine_ref[...]
    even = jnp.where(core_ref[0] == 0, mine, theirs)
    odd = jnp.where(core_ref[0] == 0, theirs, mine)
    pieces = []
    for x in range(X):
        pieces += [even[x * Z : (x + 1) * Z], odd[x * Z : (x + 1) * Z]]
    out_ref[...] = jnp.concatenate(pieces, axis=0).astype(BF16)


def spread(queries):
    return pl.pallas_call(
        spread_kernel,
        out_shape=jax.ShapeDtypeStruct((CHIPS, 8, WIDTH), BF16),
        in_specs=[VMEM],
        out_specs=VMEM,
        compiler_params=PARAMS,
    )(queries)


PREPARED = [
    ((KEYS, 2 * HD), BF16),
    ((KEYS, 2 * HD), BF16),
    ((2, SUFFIX + 16, 2 * HD), BF16),
    ((2, SUFFIX + 16, 2 * HD), BF16),
    ((8, 128), F32),
    ((ROWS, ROWS), BF16),
    ((ROWS, ROWS), BF16),
    ((ROWS, 128), F32),
]


def prepare(*args):
    return pl.pallas_call(
        prep_kernel,
        out_shape=[jax.ShapeDtypeStruct(*each) for each in PREPARED],
        in_specs=[SMEM] * 3 + [VMEM] * 3 + [HBM] * 7,
        out_specs=[HBM] * 8,
        scratch_shapes=[pltpu.VMEM((1024, HD), BF16)] * 8
        + [pltpu.VMEM((2, SUFFIX, HD), BF16)] * 2
        + [pltpu.VMEM(*each) for each in PREPARED]
        + [pltpu.SemaphoreType.DMA((10,)), pltpu.SemaphoreType.DMA((14,))],
        compiler_params=PARAMS,
        cost_estimate=pl.CostEstimate(flops=1, bytes_accessed=1, transcendentals=0),
    )(*args)


def attend(*args):
    return pl.pallas_call(
        attend_kernel,
        out_shape=jax.ShapeDtypeStruct((ROWS, PACKED), BF16),
        in_specs=[SMEM] + [HBM] * 9,
        out_specs=VMEM,
        scratch_shapes=[
            pltpu.VMEM((HEADS, ROWS, 2 * HD), BF16),
            pltpu.VMEM((ROWS, 128), F32),
            pltpu.VMEM((HEADS, ROWS, 2 * HD), F32),
            pltpu.VMEM((ROWS, PACKED), BF16),
        ]
        + [pltpu.VMEM(*each) for each in PREPARED]
        + [pltpu.VMEM((ROWS, WIDTH), BF16), pltpu.SemaphoreType.DMA((9,))],
        compiler_params=pltpu.CompilerParams(vmem_limit_bytes=62_800_000),
    )(*args)


def local(
    queries,
    prompt_keys,
    prompt_values,
    pool_keys,
    pool_values,
    suffix_keys,
    suffix_values,
    new_keys,
    new_values,
    suffix_lengths,
    branch_group,
    page_list,
    out_weight,
):
    page, rank = lax.axis_index("page"), lax.axis_index("tensor").reshape(1)
    core, chip = lax.rem(page, 2), lax.div(page, 2)
    sent, prompt_keys, pool_keys, prompt_values, pool_values = lax.optimization_barrier(
        (spread(queries), prompt_keys, pool_keys, prompt_values, pool_values)
    )
    gathered = lax.all_to_all(sent, "page", 0, 0, tiled=True, axis_index_groups=XZ_GROUPS)
    gathered = gathered.reshape(ROWS, WIDTH)
    row_group = lax.dynamic_index_in_dim(branch_group.reshape(CHIPS, 2, 2), core, 1, keepdims=False)
    row_group = jnp.repeat(row_group.reshape(-1), 4)
    order = row_group * ROWS + jnp.arange(ROWS)
    page_ids = jnp.concatenate([page * 4 + jnp.arange(4), (page ^ 1) * 4 + jnp.arange(4)])
    matched = page_list[:, :, None] == page_ids[None, None, :]
    page_group = jnp.sum(
        jnp.where(matched, jnp.arange(page_list.shape[0])[:, None, None], 0), axis=(0, 1)
    )
    own_group = lax.dynamic_slice_in_dim(branch_group, 2 * page, 2)
    limits = jnp.concatenate(
        [page_group * ROWS, (page_group + 1) * ROWS, own_group * ROWS + chip * 8 + jnp.arange(2) * 4]
    )
    at = jnp.sum((order[:, None] < limits[None, :]).astype(jnp.int32), axis=0)
    own_pages = [prompt_keys, prompt_values, pool_keys, pool_values]
    other_pages = lax.ppermute(jnp.concatenate(own_pages, axis=0), "page", CORE_SWAP)
    def from_rank(offset, array):
        return lax.ppermute(array, "tensor", [(t, (t - offset) % T) for t in range(T)])

    weight, other_pages = lax.optimization_barrier((out_weight.T[None], other_pages))
    across, after, before = from_rank(4, weight), from_rank(2, weight), from_rank(6, weight)
    prepared = prepare(
        chip.reshape(1), page_group, suffix_lengths, row_group.reshape(1, ROWS), new_keys, new_values,
        *own_pages, other_pages, suffix_keys, suffix_values,
    )
    gathered, across = lax.optimization_barrier((gathered, across))
    packed = attend(at, *prepared, gathered)
    packed, weight = lax.optimization_barrier((packed, weight))
    two = jnp.concatenate([weight, across], axis=0)
    next_two, last_two = from_rank(1, two), from_rank(7, two)
    came_rows = lax.all_to_all(
        packed.reshape(CHIPS, 8, PACKED), "page", 0, 0, tiled=True, axis_index_groups=XZ_GROUPS
    )
    weights = [two, after, before, next_two, last_two]
    came_rows, *weights = lax.optimization_barrier((came_rows, *weights))
    rows = pl.pallas_call(
        merge_kernel,
        out_shape=jax.ShapeDtypeStruct((Z, T, HEADS, HD), BF16),
        in_specs=[VMEM],
        out_specs=VMEM,
        scratch_shapes=[pltpu.VMEM((8, HEADS, HD), F32)],
        compiler_params=SMALL,
    )(came_rows)
    rows = lax.all_to_all(
        rows.reshape(Z * T, HEADS, HD), ("page", "tensor"), 0, 0, tiled=True, axis_index_groups=ZT_GROUPS
    )
    rows = jnp.broadcast_to(rows.reshape(1, Z, T * WIDTH), (X, Z, T * WIDTH))
    rows = lax.all_to_all(rows, "page", 0, 0, tiled=True, axis_index_groups=X_GROUPS)
    rows = rows.reshape(CHIPS, T * WIDTH)
    rows_other = lax.ppermute(rows, "page", CORE_SWAP)
    columns = out_weight.shape[1]
    mine = pl.pallas_call(
        project_mine_kernel,
        out_shape=jax.ShapeDtypeStruct((CHIPS, columns), F32),
        in_specs=[SMEM] + [VMEM] * 6,
        out_specs=VMEM,
        compiler_params=SMALL,
    )(rank, rows, *weights)
    return pl.pallas_call(
        project_all_kernel,
        out_shape=jax.ShapeDtypeStruct((2 * CHIPS, columns), BF16),
        in_specs=[SMEM] * 2 + [VMEM] * 7,
        out_specs=VMEM,
        compiler_params=SMALL,
    )(rank, core.reshape(1), rows_other, *weights, mine)


def solution(mesh):
    placed = (
        P("page", None, "tensor"),
        P("page", "tensor"),
        P("page", "tensor"),
        P("page", "tensor"),
        P("page", "tensor"),
        P("page", None, "tensor"),
        P("page", None, "tensor"),
        P("page", None, "tensor"),
        P("page", None, "tensor"),
        P("page"),
        P(),
        P(),
        P("tensor", "page"),
    )
    return jax.shard_map(
        local, mesh=mesh, in_specs=placed, out_specs=P("tensor", "page"), check_vma=False
    )
```

```python
import functools
import math

import jax
import jax.numpy as jnp
from jax import lax
from jax.experimental import pallas as pl
from jax.experimental.pallas import tpu as pltpu
from jax.sharding import PartitionSpec as P

HD = 128
PAGE = 256
HEADS = 8
X, Z = 4, 8
CHIPS = X * Z
T = 8
BRANCHES = 4 * CHIPS
ROWS = CHIPS * 8
WIDTH = HEADS * HD
PACKED = WIDTH + 128
SUFFIX = 512
SCALE = math.log2(math.e) / math.sqrt(HD)
PROMPT, KEYS = 2048, 4096
WINDOW = 64
NEG = -1e30
NT = (((1,), (1,)), ((), ()))
BF16, F32 = jnp.bfloat16, jnp.float32
VMEM = pl.BlockSpec(memory_space=pltpu.VMEM)
SMEM = pl.BlockSpec(memory_space=pltpu.SMEM)
HBM = pl.BlockSpec(memory_space=pltpu.HBM)
PARAMS = pltpu.CompilerParams(vmem_limit_bytes=60 * 1024 * 1024)
SMALL = pltpu.CompilerParams(vmem_limit_bytes=8 * 1024 * 1024)


def page_id(x, z, core):
    return (x * Z + z) * 2 + core


XZ_GROUPS = [[page_id(x, z, c) for x in range(X) for z in range(Z)] for c in range(2)]
CT_GROUPS = [
    [page_id(x, z, c) * T + t for c in range(2) for t in range(T)] for x in range(X) for z in range(Z)
]
CORE_SWAP = [(p, p ^ 1) for p in range(2 * CHIPS)]


def split3(x):
    high = x.astype(BF16).astype(F32)
    rest = x - high
    middle = rest.astype(BF16).astype(F32)
    return high, middle, rest - middle


def spread_kernel(q_ref, out_ref):
    rows = jnp.concatenate([q_ref[0].astype(F32), q_ref[1].astype(F32)], axis=0).astype(BF16)
    for i in range(CHIPS):
        out_ref[i] = rows


def copies_of(pairs, sems):
    return [pltpu.make_async_copy(a, b, sems.at[i]) for i, (a, b) in enumerate(pairs)]


def prep_kernel(
    page_ref, lengths_ref, branch_group_ref, page_list_ref, new_keys_ref, new_values_ref, *refs,
):
    sources, results, at_ref, held, made = refs[:8], refs[8:16], refs[16], refs[17:27], refs[27:35]
    in_sems, out_sems = refs[35:]
    halves = [each.at[n * 1024 : (n + 1) * 1024] for each in sources[4:6] for n in range(2)]
    sources = [*sources[:4], *halves, *sources[6:]]
    suffix_keys_ref, suffix_values_ref = held[8:]
    keys_ref, values_ref, own_keys_ref, own_values_ref, longest_ref, sort_ref, unsort_ref, marks_ref = made
    incoming = copies_of(list(zip(sources, held)), in_sems)
    quarters = [slice(n * 1024, (n + 1) * 1024) for n in range(4)]
    outgoing = copies_of(
        list(zip(made[2:], results[2:]))
        + [(made[i].at[rows], results[i].at[rows]) for rows in quarters for i in (0, 1)],
        out_sems,
    )
    for copy in incoming:
        copy.start()
    lane = lax.broadcasted_iota(jnp.int32, (PAGE, 128), 1)
    ones = jnp.ones((PAGE, HD), BF16)
    down = lax.broadcasted_iota(jnp.int32, (ROWS, ROWS), 0)
    across = lax.broadcasted_iota(jnp.int32, (ROWS, ROWS), 1)
    page, core, chip = page_ref[0], lax.rem(page_ref[0], 2), lax.div(page_ref[0], 2)
    branch = lax.broadcasted_iota(jnp.int32, (BRANCHES, ROWS), 0)
    row = lax.broadcasted_iota(jnp.int32, (BRANCHES, ROWS), 1)
    its_branch = (branch == 4 * (row // 8) + 2 * core + row % 8 // 4).astype(BF16)
    branch_group = jnp.broadcast_to(branch_group_ref[...].astype(F32), (8, BRANCHES)).astype(BF16)
    group_across = jnp.dot(branch_group, its_branch, preferred_element_type=F32)[0:1].astype(jnp.int32)
    order_across = group_across * ROWS + lax.broadcasted_iota(jnp.int32, (1, ROWS), 1)

    page_list = page_list_ref[...]
    list_group = lax.broadcasted_iota(jnp.int32, page_list.shape, 0)
    groups = []
    for j in range(8):
        page_id = 4 * (page if j < 4 else page + 1 - 2 * core) + j % 4
        found = jnp.sum(jnp.where(page_list == page_id, list_group, 0), axis=0, keepdims=True)
        groups.append(jnp.sum(found, axis=1, keepdims=True))
    group_down = jnp.sum(jnp.where(down == across, group_across, 0), axis=1, keepdims=True)
    before = group_down * ROWS + down < group_across * ROWS + across
    rank = jnp.sum(before.astype(jnp.int32), axis=0, keepdims=True)
    sort = (rank == down).astype(BF16)
    sort_ref[...] = sort
    same = (down == across).astype(BF16)
    unsort_ref[...] = lax.dot_general(same, sort, NT, preferred_element_type=F32).astype(BF16)
    mark = lax.broadcasted_iota(jnp.int32, (ROWS, 128), 1)
    place = lax.broadcasted_iota(jnp.int32, (ROWS, 128), 0) - chip * 8
    own = (place >= 0) & (place < 8)
    marks = (mark == 16 + group_down) | (own & (mark == 32 + place)) | (jnp.logical_not(own) & (mark == 40))
    marks_ref[...] = jnp.dot(sort, marks.astype(BF16), preferred_element_type=F32)
    for copy in outgoing[3:6]:
        copy.start()
    longest = jnp.zeros((PAGE, 1), F32)
    for n, group_at in ((0, None), (2, 0), (1, None), (3, 4)):
        source = (0, 4, 2, 6)[n]
        incoming[source].wait()
        incoming[source + 1].wait()
        for j in range(4):
            rows = slice((4 * n + j) * PAGE, (4 * n + j + 1) * PAGE)
            key = held[source][j * PAGE : (j + 1) * PAGE, :]
            wide = key.astype(F32)
            longest = jnp.maximum(longest, jnp.sum(wide * wide, axis=1, keepdims=True))
            more = (lane < 8).astype(F32)
            if group_at is not None:
                hidden = (lane >= 16) & (lane < 32) & (lane != 16 + groups[group_at + j])
                more = jnp.where(hidden, NEG, more)
            keys_ref[rows, :HD] = key
            keys_ref[rows, HD:] = more.astype(BF16)
            values_ref[rows, :HD] = held[source + 1][j * PAGE : (j + 1) * PAGE, :]
            values_ref[rows, HD:] = ones
        outgoing[6 + 2 * n].start()
        outgoing[7 + 2 * n].start()
    incoming[8].wait()
    incoming[9].wait()
    new_lane = lax.broadcasted_iota(jnp.int32, (16, 128), 1)
    new_token = lax.broadcasted_iota(jnp.int32, (16, 128), 0)
    blank = jnp.zeros((12, HD), F32)
    longest_own = longest
    for j in range(2):
        here = (lane >= 32 + 4 * j) & (lane < 36 + 4 * j)
        other_row = (lane >= 32) & (lane <= 40) & jnp.logical_not(here)
        for n in range(SUFFIX // PAGE):
            rows = slice(n * PAGE, (n + 1) * PAGE)
            token = lax.broadcasted_iota(jnp.int32, (PAGE, 128), 0) + n * PAGE
            hidden = other_row | (here & (token >= lengths_ref[j]))
            key = suffix_keys_ref[j, rows, :]
            wide = key.astype(F32)
            longest_own = jnp.maximum(longest_own, jnp.sum(wide * wide, axis=1, keepdims=True))
            own_keys_ref[j, rows, :HD] = key
            own_keys_ref[j, rows, HD:] = jnp.where(hidden, NEG, (lane < 8).astype(F32)).astype(BF16)
            own_values_ref[j, rows, :HD] = suffix_values_ref[j, rows, :]
            own_values_ref[j, rows, HD:] = ones
        seen = (new_lane >= 32 + 4 * j) & (new_lane < 36 + 4 * j) & (new_token <= new_lane - (32 + 4 * j))
        hidden = (new_lane >= 32) & (new_lane <= 40) & jnp.logical_not(seen)
        wide = new_keys_ref[j].astype(F32)
        longest_own = jnp.maximum(longest_own, jnp.max(jnp.sum(wide * wide, axis=1, keepdims=True)))
        own_keys_ref[j, SUFFIX:, :HD] = jnp.concatenate([wide, blank], axis=0).astype(BF16)
        own_keys_ref[j, SUFFIX:, HD:] = jnp.where(hidden, NEG, (new_lane < 8).astype(F32)).astype(BF16)
        own_values_ref[j, SUFFIX:, :HD] = jnp.concatenate([new_values_ref[j].astype(F32), blank], axis=0).astype(BF16)
        own_values_ref[j, SUFFIX:, HD:] = ones[:16]
    longest_ref[0:1, :] = jnp.broadcast_to(jnp.sqrt(jnp.max(longest)) * 1.02, (1, 128))
    longest_ref[1:2, :] = jnp.broadcast_to(jnp.sqrt(jnp.max(longest_own)) * 1.02, (1, 128))
    longest_ref[2:8, :] = jnp.zeros((6, 128), F32)
    for copy in outgoing[:3]:
        copy.start()
    own_row = lax.broadcasted_iota(jnp.int32, (1, ROWS), 1) - chip * 8
    limits = [group * ROWS for group in groups] + [(group + 1) * ROWS for group in groups]
    for j in range(2):
        limits.append(jnp.sum(jnp.where(own_row == 4 * j, order_across, 0), axis=1, keepdims=True))
    below = [jnp.sum((order_across < limit).astype(jnp.int32), axis=1, keepdims=True) for limit in limits]
    for j in range(18):
        at_ref[j] = below[j][0, 0]
    for copy in outgoing:
        copy.wait()


def attend_kernel(
    at_ref, q_ref, *refs,
):
    sources, out_ref, (q_rows, shift_ref, total_ref, sent_ref), held, sems = (
        refs[:8], refs[8], refs[9:13], refs[13:21], refs[21]
    )
    keys_ref, values_ref, own_keys_ref, own_values_ref, longest_ref, sort_ref, unsort_ref, marks_ref = held
    first, later = pl.ds(0, PROMPT), pl.ds(PROMPT, KEYS - PROMPT)
    pairs = list(zip(sources, held))
    pairs = [pairs[5], pairs[7], pairs[4]] + [
        (a.at[rows], b.at[rows]) for rows in (first, later) for a, b in pairs[:2]
    ] + [pairs[2], pairs[3], pairs[6]]
    copies = copies_of(pairs, sems)
    for copy in copies:
        copy.start()
    for copy in copies[:3]:
        copy.wait()
    lane = lax.broadcasted_iota(jnp.int32, (ROWS, 128), 1)
    q_all = jnp.dot(sort_ref[...], q_ref[...], preferred_element_type=F32)
    by_head = lax.broadcasted_iota(jnp.int32, (WIDTH, 128), 0) // HD == lax.broadcasted_iota(jnp.int32, (WIDTH, 128), 1)
    squares = jnp.dot((q_all * q_all).astype(BF16), by_head.astype(BF16), preferred_element_type=F32)
    marks = marks_ref[...]
    longest = jnp.where(marks[:, 40:41] > 0.5, longest_ref[0:1, :], longest_ref[1:2, :])
    shift = (jnp.sqrt(squares) * longest).astype(BF16).astype(F32)
    shift_ref[...] = shift
    for h in range(HEADS):
        q_rows[h, :, :HD] = q_all[:, h * HD : (h + 1) * HD].astype(BF16)
        q_rows[h, :, HD:] = jnp.where(lane == h, -shift, marks).astype(BF16)

    def powers(q, keys, more=0.0):
        return jnp.exp2(lax.dot_general(q, keys, NT, preferred_element_type=F32) * SCALE + more).astype(BF16)

    def taken(j, row, size, keys, values, more=0.0):
        rows = pl.ds(pl.multiple_of(row, 16), size)
        q = q_rows[:, rows, :].reshape(HEADS * size, 2 * HD)
        return rows, size, jnp.dot(powers(q, keys, more), values, preferred_element_type=F32)

    def add(rows, size, added):
        total_ref[:, rows, :] += added.reshape(HEADS, size, 2 * HD)

    def page(j):
        return pl.ds(pl.multiple_of(PROMPT + j * PAGE, PAGE), PAGE)

    for copy in copies[3:5]:
        copy.wait()
    for h in range(HEADS):
        power = powers(q_rows[h], keys_ref[:PROMPT, :])
        total_ref[h] = jnp.dot(power, values_ref[:PROMPT, :], preferred_element_type=F32)
    for copy in copies[5:]:
        copy.wait()
    firsts = [jnp.minimum(lax.div(at_ref[j], 16) * 16, ROWS - WINDOW) for j in range(8)]
    parts = [taken(j, firsts[j], WINDOW, keys_ref[page(j), :], values_ref[page(j), :]) for j in range(8)]
    parts += [
        taken(j, lax.div(at_ref[16 + j], 16) * 16, 16, own_keys_ref[j], own_values_ref[j]) for j in range(2)
    ]
    for part in parts:
        add(*part)

    def rest(j, _):
        first = jnp.minimum(lax.div(at_ref[j], 16) * 16, ROWS - WINDOW) + WINDOW
        left = at_ref[8 + j] - first

        def more_rows(i, _):
            wanted = first + i * WINDOW
            row = jnp.minimum(wanted, ROWS - WINDOW)
            done = lax.broadcasted_iota(jnp.int32, (HEADS, WINDOW, 1), 1) + row < wanted
            hide = jnp.where(done, NEG, 0.0).reshape(HEADS * WINDOW, 1)
            add(*taken(j, row, WINDOW, keys_ref[page(j), :], values_ref[page(j), :], hide))
            return 0

        lax.fori_loop(0, jnp.where(left > 0, lax.div(left + WINDOW - 1, WINDOW), 0), more_rows, 0)
        return 0

    lax.fori_loop(0, 8, rest, 0)

    def masses():
        mass = jnp.ones((ROWS, 128), F32)
        for h in range(HEADS):
            mass = jnp.where(lane == h, total_ref[h, :, HD:], mass)
        return mass

    @pl.when(jnp.min(masses()) < 2.0**-90)
    def _():
        def one_head(h, _):
            def scores(keys):
                return lax.dot_general(q_rows[h], keys, NT, preferred_element_type=F32)

            def some(c):
                return pl.ds(pl.multiple_of(c * 1024, 1024), 1024)

            def peak_of(c, peak):
                return jnp.maximum(peak, jnp.max(scores(keys_ref[some(c), :]), axis=1, keepdims=True))

            peak = lax.fori_loop(0, KEYS // 1024, peak_of, jnp.full((ROWS, 1), -3e38, F32))
            for j in range(2):
                peak = jnp.maximum(peak, jnp.max(scores(own_keys_ref[j]), axis=1, keepdims=True))
            total_ref[h] = jnp.zeros((ROWS, 2 * HD), F32)

            def add_some(keys, values):
                power = jnp.exp2((scores(keys) - peak) * SCALE).astype(BF16)
                total_ref[h] += jnp.dot(power, values, preferred_element_type=F32)

            def add_chunk(c, _):
                add_some(keys_ref[some(c), :], values_ref[some(c), :])
                return 0

            lax.fori_loop(0, KEYS // 1024, add_chunk, 0)
            for j in range(2):
                add_some(own_keys_ref[j], own_values_ref[j])
            shift_ref[...] += jnp.where(lane == h, peak, 0.0)
            return 0

        lax.fori_loop(0, HEADS, one_head, 0)

    for h in range(HEADS):
        sent_ref[:, h * HD : (h + 1) * HD] = (total_ref[h, :, :HD] / total_ref[h, :, HD:]).astype(BF16)
    lse = jnp.where(lane < HEADS, shift_ref[...] * SCALE + jnp.log2(masses()), 0.0)
    high, middle, low = split3(lse)
    sent_ref[:, WIDTH:] = (high + pltpu.roll(middle, 8, 1) + pltpu.roll(low, 16, 1)).astype(BF16)
    out_ref[...] = jnp.dot(unsort_ref[...], sent_ref[...], preferred_element_type=F32).astype(BF16)


def merge_kernel(came_ref, out_ref, rows_ref):
    parts = came_ref[:, :, WIDTH:].astype(F32)
    lse = parts + pltpu.roll(parts, 120, 2) + pltpu.roll(parts, 112, 2)
    top = jnp.max(lse, axis=0, keepdims=True)
    weights = jnp.exp2(lse - top)
    weights = weights / jnp.sum(weights, axis=0, keepdims=True)
    for h in range(HEADS):
        cols = slice(h * HD, (h + 1) * HD)
        rows_ref[:, cols] = jnp.sum(came_ref[:, :, cols].astype(F32) * weights[:, :, h : h + 1], axis=0)
    rows = rows_ref[...].astype(BF16)
    for i in range(CHIPS):
        out_ref[i] = rows


def project_kernel(core_ref, rows_ref, mine_ref, other_ref, out_ref):
    rows = rows_ref[...]
    mine = lax.dot_general(rows, mine_ref[...], NT, preferred_element_type=F32)
    other = lax.dot_general(rows, other_ref[...], NT, preferred_element_type=F32)
    first = core_ref[0] == 0
    for c, block in enumerate((jnp.where(first, mine, other), jnp.where(first, other, mine))):
        for t in range(T):
            out_ref[c * T + t] = block[t * CHIPS : (t + 1) * CHIPS].astype(BF16)


def total_kernel(shares_ref, out_ref):
    halves = [jnp.sum(shares_ref[c * T : (c + 1) * T].astype(F32), axis=0) for c in range(2)]
    pieces = [halves[c][i * 8 : (i + 1) * 8] for i in range(CHIPS // 8) for c in range(2)]
    out_ref[...] = jnp.concatenate(pieces, axis=0).astype(BF16)


def spread(queries):
    return pl.pallas_call(
        spread_kernel,
        out_shape=jax.ShapeDtypeStruct((CHIPS, 8, WIDTH), BF16),
        in_specs=[VMEM],
        out_specs=VMEM,
        compiler_params=PARAMS,
    )(queries)


PREPARED = [
    ((KEYS, 2 * HD), BF16),
    ((KEYS, 2 * HD), BF16),
    ((2, SUFFIX + 16, 2 * HD), BF16),
    ((2, SUFFIX + 16, 2 * HD), BF16),
    ((8, 128), F32),
    ((ROWS, ROWS), BF16),
    ((ROWS, ROWS), BF16),
    ((ROWS, 128), F32),
]


def prepare(*args):
    return pl.pallas_call(
        prep_kernel,
        out_shape=[jax.ShapeDtypeStruct(*each) for each in PREPARED] + [jax.ShapeDtypeStruct((18,), jnp.int32)],
        in_specs=[SMEM] * 2 + [VMEM] * 4 + [HBM] * 8,
        out_specs=[HBM] * 8 + [SMEM],
        scratch_shapes=[pltpu.VMEM((1024, HD), BF16)] * 8
        + [pltpu.VMEM((2, SUFFIX, HD), BF16)] * 2
        + [pltpu.VMEM(*each) for each in PREPARED]
        + [pltpu.SemaphoreType.DMA((10,)), pltpu.SemaphoreType.DMA((14,))],
        compiler_params=PARAMS,
        cost_estimate=pl.CostEstimate(flops=1, bytes_accessed=1, transcendentals=0),
    )(*args)


def attend(*args):
    return pl.pallas_call(
        attend_kernel,
        out_shape=jax.ShapeDtypeStruct((ROWS, PACKED), BF16),
        in_specs=[SMEM, VMEM] + [HBM] * 8,
        out_specs=VMEM,
        scratch_shapes=[
            pltpu.VMEM((HEADS, ROWS, 2 * HD), BF16),
            pltpu.VMEM((ROWS, 128), F32),
            pltpu.VMEM((HEADS, ROWS, 2 * HD), F32),
            pltpu.VMEM((ROWS, PACKED), BF16),
        ]
        + [pltpu.VMEM(*each) for each in PREPARED]
        + [pltpu.SemaphoreType.DMA((10,))],
        compiler_params=PARAMS,
    )(*args)


def local(
    queries,
    prompt_keys,
    prompt_values,
    pool_keys,
    pool_values,
    suffix_keys,
    suffix_values,
    new_keys,
    new_values,
    suffix_lengths,
    branch_group,
    page_list,
    out_weight,
):
    page = lax.axis_index("page")
    core = lax.rem(page, 2)
    sent, prompt_keys, pool_keys, prompt_values, pool_values = lax.optimization_barrier(
        (spread(queries), prompt_keys, pool_keys, prompt_values, pool_values)
    )
    gathered = lax.all_to_all(sent, "page", 0, 0, tiled=True, axis_index_groups=XZ_GROUPS)
    gathered = gathered.reshape(ROWS, WIDTH)
    own_pages = [prompt_keys, prompt_values, pool_keys, pool_values]
    pairs = [jnp.concatenate(pair, axis=0) for pair in ((prompt_keys, prompt_values), (pool_keys, pool_values))]
    other_pages = [lax.ppermute(pair, "page", CORE_SWAP) for pair in pairs]
    *prepared, at = prepare(
        page.reshape(1), suffix_lengths, branch_group.reshape(1, BRANCHES), page_list, new_keys, new_values,
        *own_pages, *other_pages, suffix_keys, suffix_values,
    )
    packed = attend(at, gathered, *prepared)
    packed, weight = lax.optimization_barrier((packed, out_weight.T))
    other_weight = lax.ppermute(weight, "page", CORE_SWAP)
    came = lax.all_to_all(
        packed.reshape(CHIPS, 8, PACKED), "page", 0, 0, tiled=True, axis_index_groups=XZ_GROUPS
    )
    came, other_weight = lax.optimization_barrier((came, other_weight))
    rows = pl.pallas_call(
        merge_kernel,
        out_shape=jax.ShapeDtypeStruct((CHIPS, 8, WIDTH), BF16),
        in_specs=[VMEM],
        out_specs=VMEM,
        scratch_shapes=[pltpu.VMEM((8, WIDTH), F32)],
        compiler_params=SMALL,
    )(came)
    rows = lax.all_to_all(rows, "page", 0, 0, tiled=True, axis_index_groups=XZ_GROUPS)
    columns = out_weight.shape[1]
    shares = pl.pallas_call(
        project_kernel,
        out_shape=jax.ShapeDtypeStruct((2 * T, CHIPS, columns), BF16),
        in_specs=[SMEM] + [VMEM] * 3,
        out_specs=VMEM,
        compiler_params=SMALL,
    )(core.reshape(1), rows.reshape(ROWS, WIDTH), weight, other_weight)
    shares = lax.all_to_all(shares, ("page", "tensor"), 0, 0, tiled=True, axis_index_groups=CT_GROUPS)
    return pl.pallas_call(
        total_kernel,
        out_shape=jax.ShapeDtypeStruct((2 * CHIPS, columns), BF16),
        in_specs=[VMEM],
        out_specs=VMEM,
        compiler_params=SMALL,
    )(shares)


def solution(mesh):
    placed = (
        P("page", None, "tensor"),
        P("page", "tensor"),
        P("page", "tensor"),
        P("page", "tensor"),
        P("page", "tensor"),
        P("page", None, "tensor"),
        P("page", None, "tensor"),
        P("page", None, "tensor"),
        P("page", None, "tensor"),
        P("page"),
        P(),
        P(),
        P("tensor", "page"),
    )
    return jax.shard_map(
        local, mesh=mesh, in_specs=placed, out_specs=P("tensor", "page"), check_vma=False
    )
```

```python
import functools
import math

import jax
import jax.numpy as jnp
from jax import lax
from jax.experimental import pallas as pl
from jax.experimental.pallas import tpu as pltpu
from jax.sharding import PartitionSpec as P

HD = 128
PAGE = 256
HEADS = 8
X, Z = 4, 8
CHIPS = X * Z
T = 8
BRANCHES = 4 * CHIPS
ROWS = CHIPS * 8
WIDTH = HEADS * HD
PACKED = WIDTH + 128
SUFFIX = 512
SCALE = math.log2(math.e) / math.sqrt(HD)
PROMPT, KEYS = 2048, 4096
WINDOW = 64
NEG = -1e30
NT = (((1,), (1,)), ((), ()))
BF16, F32 = jnp.bfloat16, jnp.float32
VMEM = pl.BlockSpec(memory_space=pltpu.VMEM)
SMEM = pl.BlockSpec(memory_space=pltpu.SMEM)
HBM = pl.BlockSpec(memory_space=pltpu.HBM)
PARAMS = pltpu.CompilerParams(vmem_limit_bytes=60 * 1024 * 1024)
SMALL = pltpu.CompilerParams(vmem_limit_bytes=8 * 1024 * 1024)


def page_id(x, z, core):
    return (x * Z + z) * 2 + core


XZ_GROUPS = [[page_id(x, z, c) for x in range(X) for z in range(Z)] for c in range(2)]
CT_GROUPS = [
    [page_id(x, z, c) * T + t for c in range(2) for t in range(T)] for x in range(X) for z in range(Z)
]
CORE_SWAP = [(p, p ^ 1) for p in range(2 * CHIPS)]


def split3(x):
    high = x.astype(BF16).astype(F32)
    rest = x - high
    middle = rest.astype(BF16).astype(F32)
    return high, middle, rest - middle


def spread_kernel(q_ref, out_ref):
    rows = jnp.concatenate([q_ref[0].astype(F32), q_ref[1].astype(F32)], axis=0).astype(BF16)
    for i in range(CHIPS):
        out_ref[i] = rows


def copies_of(pairs, sems):
    return [pltpu.make_async_copy(a, b, sems.at[i]) for i, (a, b) in enumerate(pairs)]


def prep_kernel(
    page_ref, lengths_ref, branch_group_ref, page_list_ref, new_keys_ref, new_values_ref, *refs,
):
    sources, results, at_ref, held, made = refs[:8], refs[8:16], refs[16], refs[17:27], refs[27:35]
    in_sems, out_sems = refs[35:]
    halves = [each.at[n * 1024 : (n + 1) * 1024] for each in sources[4:6] for n in range(2)]
    sources = [*sources[:4], *halves, *sources[6:]]
    suffix_keys_ref, suffix_values_ref = held[8:]
    keys_ref, values_ref, own_keys_ref, own_values_ref, longest_ref, sort_ref, unsort_ref, marks_ref = made
    incoming = copies_of(list(zip(sources, held)), in_sems)
    quarters = [slice(n * 1024, (n + 1) * 1024) for n in range(4)]
    outgoing = copies_of(
        list(zip(made[2:], results[2:]))
        + [(made[i].at[rows], results[i].at[rows]) for rows in quarters for i in (0, 1)],
        out_sems,
    )
    for copy in incoming:
        copy.start()
    lane = lax.broadcasted_iota(jnp.int32, (PAGE, 128), 1)
    ones = jnp.ones((PAGE, HD), BF16)
    down = lax.broadcasted_iota(jnp.int32, (ROWS, ROWS), 0)
    across = lax.broadcasted_iota(jnp.int32, (ROWS, ROWS), 1)
    page, core, chip = page_ref[0], lax.rem(page_ref[0], 2), lax.div(page_ref[0], 2)
    branch = lax.broadcasted_iota(jnp.int32, (BRANCHES, ROWS), 0)
    row = lax.broadcasted_iota(jnp.int32, (BRANCHES, ROWS), 1)
    its_branch = (branch == 4 * (row // 8) + 2 * core + row % 8 // 4).astype(BF16)
    branch_group = jnp.broadcast_to(branch_group_ref[...].astype(F32), (8, BRANCHES)).astype(BF16)
    group_across = jnp.dot(branch_group, its_branch, preferred_element_type=F32)[0:1].astype(jnp.int32)
    order_across = group_across * ROWS + lax.broadcasted_iota(jnp.int32, (1, ROWS), 1)

    page_list = page_list_ref[...]
    list_group = lax.broadcasted_iota(jnp.int32, page_list.shape, 0)
    groups = []
    for j in range(8):
        page_id = 4 * (page if j < 4 else page + 1 - 2 * core) + j % 4
        found = jnp.sum(jnp.where(page_list == page_id, list_group, 0), axis=0, keepdims=True)
        groups.append(jnp.sum(found, axis=1, keepdims=True))
    group_down = jnp.sum(jnp.where(down == across, group_across, 0), axis=1, keepdims=True)
    before = group_down * ROWS + down < group_across * ROWS + across
    rank = jnp.sum(before.astype(jnp.int32), axis=0, keepdims=True)
    sort = (rank == down).astype(BF16)
    sort_ref[...] = sort
    same = (down == across).astype(BF16)
    unsort_ref[...] = lax.dot_general(same, sort, NT, preferred_element_type=F32).astype(BF16)
    mark = lax.broadcasted_iota(jnp.int32, (ROWS, 128), 1)
    place = lax.broadcasted_iota(jnp.int32, (ROWS, 128), 0) - chip * 8
    own = (place >= 0) & (place < 8)
    marks = (mark == 16 + group_down) | (own & (mark == 32 + place)) | (jnp.logical_not(own) & (mark == 40))
    marks_ref[...] = jnp.dot(sort, marks.astype(BF16), preferred_element_type=F32)
    for copy in outgoing[3:6]:
        copy.start()
    longest = jnp.zeros((PAGE, 1), F32)
    for n, group_at in ((0, None), (2, 0), (1, None), (3, 4)):
        source = (0, 4, 2, 6)[n]
        incoming[source].wait()
        incoming[source + 1].wait()
        for j in range(4):
            rows = slice((4 * n + j) * PAGE, (4 * n + j + 1) * PAGE)
            key = held[source][j * PAGE : (j + 1) * PAGE, :]
            wide = key.astype(F32)
            longest = jnp.maximum(longest, jnp.sum(wide * wide, axis=1, keepdims=True))
            more = (lane < 8).astype(F32)
            if group_at is not None:
                hidden = (lane >= 16) & (lane < 32) & (lane != 16 + groups[group_at + j])
                more = jnp.where(hidden, NEG, more)
            keys_ref[rows, :HD] = key
            keys_ref[rows, HD:] = more.astype(BF16)
            values_ref[rows, :HD] = held[source + 1][j * PAGE : (j + 1) * PAGE, :]
            values_ref[rows, HD:] = ones
        outgoing[6 + 2 * n].start()
        outgoing[7 + 2 * n].start()
    incoming[8].wait()
    incoming[9].wait()
    new_lane = lax.broadcasted_iota(jnp.int32, (16, 128), 1)
    new_token = lax.broadcasted_iota(jnp.int32, (16, 128), 0)
    blank = jnp.zeros((12, HD), F32)
    longest_own = longest
    for j in range(2):
        here = (lane >= 32 + 4 * j) & (lane < 36 + 4 * j)
        other_row = (lane >= 32) & (lane <= 40) & jnp.logical_not(here)
        for n in range(SUFFIX // PAGE):
            rows = slice(n * PAGE, (n + 1) * PAGE)
            token = lax.broadcasted_iota(jnp.int32, (PAGE, 128), 0) + n * PAGE
            hidden = other_row | (here & (token >= lengths_ref[j]))
            key = suffix_keys_ref[j, rows, :]
            wide = key.astype(F32)
            longest_own = jnp.maximum(longest_own, jnp.sum(wide * wide, axis=1, keepdims=True))
            own_keys_ref[j, rows, :HD] = key
            own_keys_ref[j, rows, HD:] = jnp.where(hidden, NEG, (lane < 8).astype(F32)).astype(BF16)
            own_values_ref[j, rows, :HD] = suffix_values_ref[j, rows, :]
            own_values_ref[j, rows, HD:] = ones
        seen = (new_lane >= 32 + 4 * j) & (new_lane < 36 + 4 * j) & (new_token <= new_lane - (32 + 4 * j))
        hidden = (new_lane >= 32) & (new_lane <= 40) & jnp.logical_not(seen)
        wide = new_keys_ref[j].astype(F32)
        longest_own = jnp.maximum(longest_own, jnp.max(jnp.sum(wide * wide, axis=1, keepdims=True)))
        own_keys_ref[j, SUFFIX:, :HD] = jnp.concatenate([wide, blank], axis=0).astype(BF16)
        own_keys_ref[j, SUFFIX:, HD:] = jnp.where(hidden, NEG, (new_lane < 8).astype(F32)).astype(BF16)
        own_values_ref[j, SUFFIX:, :HD] = jnp.concatenate([new_values_ref[j].astype(F32), blank], axis=0).astype(BF16)
        own_values_ref[j, SUFFIX:, HD:] = ones[:16]
    longest_ref[0:1, :] = jnp.broadcast_to(jnp.sqrt(jnp.max(longest)) * 1.02, (1, 128))
    longest_ref[1:2, :] = jnp.broadcast_to(jnp.sqrt(jnp.max(longest_own)) * 1.02, (1, 128))
    longest_ref[2:8, :] = jnp.zeros((6, 128), F32)
    for copy in outgoing[:3]:
        copy.start()
    own_row = lax.broadcasted_iota(jnp.int32, (1, ROWS), 1) - chip * 8
    limits = [group * ROWS for group in groups] + [(group + 1) * ROWS for group in groups]
    for j in range(2):
        limits.append(jnp.sum(jnp.where(own_row == 4 * j, order_across, 0), axis=1, keepdims=True))
    below = [jnp.sum((order_across < limit).astype(jnp.int32), axis=1, keepdims=True) for limit in limits]
    for j in range(18):
        at_ref[j] = below[j][0, 0]
    for copy in outgoing:
        copy.wait()


def attend_kernel(
    at_ref, *refs,
):
    sources, out_ref, (q_rows, shift_ref, total_ref, sent_ref), held, sems = (
        refs[:9], refs[9], refs[10:14], refs[14:23], refs[23]
    )
    q_ref, keys_ref, values_ref, own_keys_ref, own_values_ref, longest_ref, sort_ref, unsort_ref, marks_ref = held
    first, later = pl.ds(0, PROMPT), pl.ds(PROMPT, KEYS - PROMPT)
    pairs = list(zip(sources, held))
    pairs = [pairs[0], pairs[6], pairs[8], pairs[5]] + [
        (a.at[rows], b.at[rows]) for rows in (first, later) for a, b in pairs[1:3]
    ] + [pairs[3], pairs[4], pairs[7]]
    copies = copies_of(pairs, sems)
    for copy in copies:
        copy.start()
    for copy in copies[:4]:
        copy.wait()
    lane = lax.broadcasted_iota(jnp.int32, (ROWS, 128), 1)
    q_all = jnp.dot(sort_ref[...], q_ref[...], preferred_element_type=F32)
    by_head = lax.broadcasted_iota(jnp.int32, (WIDTH, 128), 0) // HD == lax.broadcasted_iota(jnp.int32, (WIDTH, 128), 1)
    squares = jnp.dot((q_all * q_all).astype(BF16), by_head.astype(BF16), preferred_element_type=F32)
    marks = marks_ref[...]
    longest = jnp.where(marks[:, 40:41] > 0.5, longest_ref[0:1, :], longest_ref[1:2, :])
    shift = (jnp.sqrt(squares) * longest).astype(BF16).astype(F32)
    shift_ref[...] = shift
    for h in range(HEADS):
        q_rows[h, :, :HD] = q_all[:, h * HD : (h + 1) * HD].astype(BF16)
        q_rows[h, :, HD:] = jnp.where(lane == h, -shift, marks).astype(BF16)

    def powers(q, keys, more=0.0):
        return jnp.exp2(lax.dot_general(q, keys, NT, preferred_element_type=F32) * SCALE + more).astype(BF16)

    def taken(j, row, size, keys, values, more=0.0):
        rows = pl.ds(pl.multiple_of(row, 16), size)
        q = q_rows[:, rows, :].reshape(HEADS * size, 2 * HD)
        return rows, size, jnp.dot(powers(q, keys, more), values, preferred_element_type=F32)

    def add(rows, size, added):
        total_ref[:, rows, :] += added.reshape(HEADS, size, 2 * HD)

    def page(j):
        return pl.ds(pl.multiple_of(PROMPT + j * PAGE, PAGE), PAGE)

    for copy in copies[4:6]:
        copy.wait()
    for h in range(HEADS):
        power = powers(q_rows[h], keys_ref[:PROMPT, :])
        total_ref[h] = jnp.dot(power, values_ref[:PROMPT, :], preferred_element_type=F32)
    for copy in copies[6:]:
        copy.wait()
    firsts = [jnp.minimum(lax.div(at_ref[j], 16) * 16, ROWS - WINDOW) for j in range(8)]
    parts = [taken(j, firsts[j], WINDOW, keys_ref[page(j), :], values_ref[page(j), :]) for j in range(8)]
    parts += [
        taken(j, lax.div(at_ref[16 + j], 16) * 16, 16, own_keys_ref[j], own_values_ref[j]) for j in range(2)
    ]
    for part in parts:
        add(*part)

    def rest(j, _):
        first = jnp.minimum(lax.div(at_ref[j], 16) * 16, ROWS - WINDOW) + WINDOW
        left = at_ref[8 + j] - first

        def more_rows(i, _):
            wanted = first + i * WINDOW
            row = jnp.minimum(wanted, ROWS - WINDOW)
            done = lax.broadcasted_iota(jnp.int32, (HEADS, WINDOW, 1), 1) + row < wanted
            hide = jnp.where(done, NEG, 0.0).reshape(HEADS * WINDOW, 1)
            add(*taken(j, row, WINDOW, keys_ref[page(j), :], values_ref[page(j), :], hide))
            return 0

        lax.fori_loop(0, jnp.where(left > 0, lax.div(left + WINDOW - 1, WINDOW), 0), more_rows, 0)
        return 0

    lax.fori_loop(0, 8, rest, 0)

    def masses():
        mass = jnp.ones((ROWS, 128), F32)
        for h in range(HEADS):
            mass = jnp.where(lane == h, total_ref[h, :, HD:], mass)
        return mass

    @pl.when(jnp.min(masses()) < 2.0**-90)
    def _():
        def one_head(h, _):
            def scores(keys):
                return lax.dot_general(q_rows[h], keys, NT, preferred_element_type=F32)

            def some(c):
                return pl.ds(pl.multiple_of(c * 1024, 1024), 1024)

            def peak_of(c, peak):
                return jnp.maximum(peak, jnp.max(scores(keys_ref[some(c), :]), axis=1, keepdims=True))

            peak = lax.fori_loop(0, KEYS // 1024, peak_of, jnp.full((ROWS, 1), -3e38, F32))
            for j in range(2):
                peak = jnp.maximum(peak, jnp.max(scores(own_keys_ref[j]), axis=1, keepdims=True))
            total_ref[h] = jnp.zeros((ROWS, 2 * HD), F32)

            def add_some(keys, values):
                power = jnp.exp2((scores(keys) - peak) * SCALE).astype(BF16)
                total_ref[h] += jnp.dot(power, values, preferred_element_type=F32)

            def add_chunk(c, _):
                add_some(keys_ref[some(c), :], values_ref[some(c), :])
                return 0

            lax.fori_loop(0, KEYS // 1024, add_chunk, 0)
            for j in range(2):
                add_some(own_keys_ref[j], own_values_ref[j])
            shift_ref[...] += jnp.where(lane == h, peak, 0.0)
            return 0

        lax.fori_loop(0, HEADS, one_head, 0)

    for h in range(HEADS):
        sent_ref[:, h * HD : (h + 1) * HD] = (total_ref[h, :, :HD] / total_ref[h, :, HD:]).astype(BF16)
    lse = jnp.where(lane < HEADS, shift_ref[...] * SCALE + jnp.log2(masses()), 0.0)
    high, middle, low = split3(lse)
    sent_ref[:, WIDTH:] = (high + pltpu.roll(middle, 8, 1) + pltpu.roll(low, 16, 1)).astype(BF16)
    out_ref[...] = jnp.dot(unsort_ref[...], sent_ref[...], preferred_element_type=F32).astype(BF16)


def merge_kernel(came_ref, out_ref, rows_ref):
    parts = came_ref[:, :, WIDTH:].astype(F32)
    lse = parts + pltpu.roll(parts, 120, 2) + pltpu.roll(parts, 112, 2)
    top = jnp.max(lse, axis=0, keepdims=True)
    weights = jnp.exp2(lse - top)
    weights = weights / jnp.sum(weights, axis=0, keepdims=True)
    for h in range(HEADS):
        cols = slice(h * HD, (h + 1) * HD)
        rows_ref[:, cols] = jnp.sum(came_ref[:, :, cols].astype(F32) * weights[:, :, h : h + 1], axis=0)
    rows = rows_ref[...].astype(BF16)
    for i in range(CHIPS):
        out_ref[i] = rows


def project_kernel(page_ref, rows_ref, mine_ref, other_ref, out_ref):
    rows = rows_ref[...]
    mine = lax.dot_general(rows, mine_ref[...], NT, preferred_element_type=F32)
    other = lax.dot_general(rows, other_ref[...], NT, preferred_element_type=F32)
    first = lax.rem(page_ref[0], 2) == 0
    for c, block in enumerate((jnp.where(first, mine, other), jnp.where(first, other, mine))):
        for t in range(T):
            out_ref[c * T + t] = block[t * CHIPS : (t + 1) * CHIPS].astype(BF16)


def total_kernel(shares_ref, out_ref):
    halves = [jnp.sum(shares_ref[c * T : (c + 1) * T].astype(F32), axis=0) for c in range(2)]
    pieces = [halves[c][i * 8 : (i + 1) * 8] for i in range(CHIPS // 8) for c in range(2)]
    out_ref[...] = jnp.concatenate(pieces, axis=0).astype(BF16)


def spread(queries):
    return pl.pallas_call(
        spread_kernel,
        out_shape=jax.ShapeDtypeStruct((CHIPS, 8, WIDTH), BF16),
        in_specs=[VMEM],
        out_specs=VMEM,
        compiler_params=PARAMS,
    )(queries)


PREPARED = [
    ((KEYS, 2 * HD), BF16),
    ((KEYS, 2 * HD), BF16),
    ((2, SUFFIX + 16, 2 * HD), BF16),
    ((2, SUFFIX + 16, 2 * HD), BF16),
    ((8, 128), F32),
    ((ROWS, ROWS), BF16),
    ((ROWS, ROWS), BF16),
    ((ROWS, 128), F32),
]


def prepare(*args):
    return pl.pallas_call(
        prep_kernel,
        out_shape=[jax.ShapeDtypeStruct(*each) for each in PREPARED] + [jax.ShapeDtypeStruct((18,), jnp.int32)],
        in_specs=[SMEM] * 2 + [VMEM] * 4 + [HBM] * 8,
        out_specs=[HBM] * 8 + [SMEM],
        scratch_shapes=[pltpu.VMEM((1024, HD), BF16)] * 8
        + [pltpu.VMEM((2, SUFFIX, HD), BF16)] * 2
        + [pltpu.VMEM(*each) for each in PREPARED]
        + [pltpu.SemaphoreType.DMA((10,)), pltpu.SemaphoreType.DMA((14,))],
        compiler_params=PARAMS,
        cost_estimate=pl.CostEstimate(flops=1, bytes_accessed=1, transcendentals=0),
    )(*args)


def attend(*args):
    return pl.pallas_call(
        attend_kernel,
        out_shape=jax.ShapeDtypeStruct((ROWS, PACKED), BF16),
        in_specs=[SMEM] + [HBM] * 9,
        out_specs=VMEM,
        scratch_shapes=[
            pltpu.VMEM((HEADS, ROWS, 2 * HD), BF16),
            pltpu.VMEM((ROWS, 128), F32),
            pltpu.VMEM((HEADS, ROWS, 2 * HD), F32),
            pltpu.VMEM((ROWS, PACKED), BF16),
        ]
        + [pltpu.VMEM((ROWS, WIDTH), BF16)]
        + [pltpu.VMEM(*each) for each in PREPARED]
        + [pltpu.SemaphoreType.DMA((11,))],
        compiler_params=PARAMS,
    )(*args)


def local(
    queries,
    prompt_keys,
    prompt_values,
    pool_keys,
    pool_values,
    suffix_keys,
    suffix_values,
    new_keys,
    new_values,
    suffix_lengths,
    branch_group,
    page_list,
    out_weight,
):
    page = lax.axis_index("page")
    sent, prompt_keys, pool_keys, prompt_values, pool_values = lax.optimization_barrier(
        (spread(queries), prompt_keys, pool_keys, prompt_values, pool_values)
    )
    gathered = lax.all_to_all(sent, "page", 0, 0, tiled=True, axis_index_groups=XZ_GROUPS)
    gathered = gathered.reshape(ROWS, WIDTH)
    own_pages = [prompt_keys, prompt_values, pool_keys, pool_values]
    pairs = [jnp.concatenate(pair, axis=0) for pair in ((prompt_keys, prompt_values), (pool_keys, pool_values))]
    other_pages = [lax.ppermute(pair, "page", CORE_SWAP) for pair in pairs]
    *prepared, at = prepare(
        page.reshape(1), suffix_lengths, branch_group.reshape(1, BRANCHES), page_list, new_keys, new_values,
        *own_pages, *other_pages, suffix_keys, suffix_values,
    )
    weight = out_weight.T
    other_weight = lax.ppermute(weight, "page", CORE_SWAP)
    gathered, other_weight = lax.optimization_barrier((gathered, other_weight))
    packed = attend(at, gathered, *prepared)
    came = lax.all_to_all(
        packed.reshape(CHIPS, 8, PACKED), "page", 0, 0, tiled=True, axis_index_groups=XZ_GROUPS
    )
    rows = pl.pallas_call(
        merge_kernel,
        out_shape=jax.ShapeDtypeStruct((CHIPS, 8, WIDTH), BF16),
        in_specs=[VMEM],
        out_specs=VMEM,
        scratch_shapes=[pltpu.VMEM((8, WIDTH), F32)],
        compiler_params=SMALL,
    )(came)
    rows = lax.all_to_all(rows, "page", 0, 0, tiled=True, axis_index_groups=XZ_GROUPS)
    columns = out_weight.shape[1]
    shares = pl.pallas_call(
        project_kernel,
        out_shape=jax.ShapeDtypeStruct((2 * T, CHIPS, columns), BF16),
        in_specs=[SMEM] + [VMEM] * 3,
        out_specs=VMEM,
        compiler_params=SMALL,
    )(page.reshape(1), rows.reshape(ROWS, WIDTH), weight, other_weight)
    shares = lax.all_to_all(shares, ("page", "tensor"), 0, 0, tiled=True, axis_index_groups=CT_GROUPS)
    return pl.pallas_call(
        total_kernel,
        out_shape=jax.ShapeDtypeStruct((2 * CHIPS, columns), BF16),
        in_specs=[VMEM],
        out_specs=VMEM,
        compiler_params=SMALL,
    )(shares)


def solution(mesh):
    placed = (
        P("page", None, "tensor"),
        P("page", "tensor"),
        P("page", "tensor"),
        P("page", "tensor"),
        P("page", "tensor"),
        P("page", None, "tensor"),
        P("page", None, "tensor"),
        P("page", None, "tensor"),
        P("page", None, "tensor"),
        P("page"),
        P(),
        P(),
        P("tensor", "page"),
    )
    return jax.shard_map(
        local, mesh=mesh, in_specs=placed, out_specs=P("tensor", "page"), check_vma=False
    )
```
